512 devices in a mesh: dp: 64 (over z, y_hi, core), replica: 8 (over x, y_lo).
Axes of the slice: x: 4, y: 8 (y_hi: 4, y_lo: 2; y = y_hi * 2 + y_lo), z: 8, core: 2. Of those that a mesh axis runs over, the one named last changes fastest.
Arguments:
- images: bfloat16 [131072, 1152], P(('dp', 'replica')), may hold values from -0.1875 to 0.1875
- texts: bfloat16 [131072, 1152], P(('dp', 'replica')), may hold values from -0.1875 to 0.1875
- head: bfloat16 [1152, 1152], P('replica'), may hold values from -0.1875 to 0.1875
- scale: float32 [1], replicated, may hold values from 10 to 30
- bias: float32 [1], replicated, may hold values from -6 to -2
- offsets: int32 [512], P(('dp', 'replica')), may hold values from 0 to 255
Outputs:
- image_grad: bfloat16 [131072, 1152], P(('dp', 'replica'))
- text_grad: bfloat16 [131072, 1152], P(('dp', 'replica'))
- head_grad: float32 [1152, 1152], P('replica')
The draws below stay inside these ranges and needn't reach their ends.
All inputs are finite; a program needn't handle non-finite values.
Results may differ from the reference program's by a relative error of at most 0.017.
Values may be sent and summed in bfloat16 or wider, within the bound.
No kernel may reach another device: no remote copies, remote signals or barrier semaphores. Data moves between devices by JAX's collectives and lax.ppermute only.
A program may use at most 64 MiB of HBM per device.

```python
import math
import jax
import jax.numpy as jnp
from jax import lax

D = 1152
ROWS_DEV = 256
STEPS = 4
SHARDS = 512
IMAGES = 131072
N_DP = 64
N_REPLICA = 8


def set_ends(array, rng, low, largest):
    longest = array.shape.index(max(array.shape))
    spots = []
    for shift in (0, 1):
        where = [jax.random.randint(jax.random.fold_in(rng, axis), (), 0, length) for axis, length in enumerate(array.shape)]
        where[longest] = (where[longest] + shift) % array.shape[longest]
        spots.append(tuple(where))
    return array.at[spots[0]].set(low).at[spots[1]].set(largest)


def block_scale(own_key, shape, split, low, largest):
    def one(dim, shards_of):
        draws = jax.random.uniform(jax.random.fold_in(jax.random.fold_in(own_key, 6), dim), (shards_of,), jnp.float32, low / len(split), largest / len(split))
        return jnp.repeat(jnp.exp(draws), shape[dim] // shards_of).reshape((-1,) + (1,) * (len(shape) - dim - 1))

    level = one(*split[0])
    for cut in split[1:]:
        level = level * one(*cut)
    return level


def noise(rng, extent, deviation, most, shards=(), kind=jnp.bfloat16):
    factor_of = block_scale(rng, extent, shards, -0.22, 0.18) if shards else 1.0
    result = jax.random.normal(rng, extent, jnp.float32) * deviation * factor_of
    return jnp.minimum(jnp.maximum(result, -most), most).astype(kind)


def setup_inputs(seed: int = 0) -> dict:
    key_list = jax.random.split(jax.random.key(seed), 7)
    return {
        "images": noise(key_list[0], (IMAGES, D), 0.03, 0.1875, ((0, 512),)),
        "texts": noise(key_list[1], (IMAGES, D), 0.03, 0.1875, ((0, 512),)),
        "head": noise(key_list[2], (D, D), D ** -0.5, 0.1875, ((0, 8),)),
        "scale": jnp.clip(jnp.exp(jax.random.uniform(key_list[3], (1,), jnp.float32, math.log(10.0), math.log(30.0))), 10.0, 30.0),
        "bias": jnp.clip(jax.random.uniform(key_list[4], (1,), jnp.float32, -6.0, -2.0), -6.0, -2.0),
        "offsets": set_ends(jax.random.randint(key_list[5], (SHARDS,), 0, ROWS_DEV), jax.random.fold_in(key_list[5], 1), 0, ROWS_DEV - 1).astype(jnp.int32),
    }


EPS = 1e-06

def unit_rows(values):
    inverse = lax.rsqrt(lax.optimization_barrier(jnp.sum(values * values, axis=-1, keepdims=True)) + EPS)
    return (values * inverse, inverse)

def coefficients(img_block, txt_block, step, offset_row, scale_value, bias_value):
    logits = scale_value * jnp.einsum('rid,rjd->rij', img_block.astype(jnp.float32), txt_block.astype(jnp.float32)) + bias_value
    count = img_block.shape[1]
    target = (jnp.arange(count, dtype=jnp.int32)[None, :] + offset_row[:, None]) % count
    positive = jnp.logical_and(jnp.arange(count, dtype=jnp.int32)[None, None, :] == target[:, :, None], step == 0)
    sign = jnp.where(positive, jnp.float32(1.0), jnp.float32(-1.0))
    coef = -sign * jax.nn.sigmoid(-sign * logits)
    return (scale_value * coef).astype(jnp.bfloat16)

def reference(images, texts, head, scale, bias, offsets):
    shape4 = (N_DP, N_REPLICA, ROWS_DEV, D)
    image_rows = images.reshape(shape4)
    text_rows = texts.reshape(shape4)
    offset_grid = offsets.reshape(N_DP, N_REPLICA)
    scale_value = scale[0]
    bias_value = bias[0]
    head32 = head.astype(jnp.float32)
    proj = jnp.einsum('abid,de->abie', image_rows.astype(jnp.float32), head32)
    img_unit, inv_img = unit_rows(proj)
    img_b = img_unit.astype(jnp.bfloat16)
    txt_unit, inv_txt = unit_rows(text_rows.astype(jnp.float32))
    txt_b = txt_unit.astype(jnp.bfloat16)

    def image_side(index):
        total = jnp.zeros((N_REPLICA, ROWS_DEV, D), jnp.float32)
        for step in range(STEPS):
            other = txt_b[(index - step) % N_DP]
            weights = coefficients(img_b[index], other, step, offset_grid[index], scale_value, bias_value)
            total = total + jnp.einsum('rij,rjd->rid', weights.astype(jnp.float32), other.astype(jnp.float32))
        return total

    def text_side(index):
        total = jnp.zeros((N_REPLICA, ROWS_DEV, D), jnp.float32)
        for step in range(STEPS):
            source = (index + step) % N_DP
            weights = coefficients(img_b[source], txt_b[index], step, offset_grid[source], scale_value, bias_value)
            part = jnp.einsum('rij,rid->rjd', weights.astype(jnp.float32), img_b[source].astype(jnp.float32)).astype(jnp.bfloat16)
            total = total + lax.optimization_barrier(part).astype(jnp.float32)
        return total
    indices = jnp.arange(N_DP, dtype=jnp.int32)
    img_dir = lax.map(image_side, indices)
    txt_dir = lax.map(text_side, indices)
    text_grad = ((txt_dir - txt_unit * lax.optimization_barrier(jnp.sum(txt_unit * txt_dir, axis=-1, keepdims=True))) * inv_txt).astype(jnp.bfloat16)
    proj_grad = ((img_dir - img_unit * lax.optimization_barrier(jnp.sum(img_unit * img_dir, axis=-1, keepdims=True))) * inv_img).astype(jnp.bfloat16)
    image_grad = jnp.einsum('abie,de->abid', proj_grad.astype(jnp.float32), head32).astype(jnp.bfloat16)

    def head_step(carry, index):
        terms = jnp.einsum('rid,rie->rde', image_rows[index].astype(jnp.float32), proj_grad[index].astype(jnp.float32)).astype(jnp.bfloat16)
        return (carry + lax.optimization_barrier(jnp.sum(lax.optimization_barrier(terms).astype(jnp.float32), axis=0)), None)
    head_grad, unused = lax.scan(head_step, jnp.zeros((D, D), jnp.float32), indices)
    return (image_grad.reshape(IMAGES, D), text_grad.reshape(IMAGES, D), head_grad)
```

```python
import jax
import jax.numpy as jnp
from jax import lax
from jax.sharding import Mesh
from jax.sharding import PartitionSpec as P

EPS = 1e-06
DP = ("z", "yh", "core")
RING = ("z", "yh")
REP = ("x", "yl")
ALL = DP + REP


def dot(a, b, ca, cb):
    return lax.dot_general(a, b, (((ca,), (cb,)), ((), ())), preferred_element_type=jnp.float32)


def by_chip(shift):
    return [(p, (p + 2 * shift) % 64) for p in range(64)]


SWAP = [(0, 1), (1, 0)]
REST = [(p, p + 1) if p % 2 == 0 else (p, (p + 3) % 64) for p in range(64)]
REST_BACK = [(b, a) for a, b in REST]


def exchange(array, axes):
    return lax.all_to_all(array, axes, split_axis=0, concat_axis=0, tiled=True)


def spread(array, axes, count):
    return exchange(jnp.broadcast_to(array[None], (count,) + array.shape), axes)


def unit_rows(values):
    inverse = lax.rsqrt(jnp.sum(values * values, axis=-1, keepdims=True) + EPS)
    return values * inverse, inverse


def weights_of(img_b, other, scale, bias, target=None):
    logits = scale * dot(img_b, other, 1, 1) + bias
    if target is None:
        return (scale * jax.nn.sigmoid(logits)).astype(jnp.bfloat16)
    count = img_b.shape[0]
    positive = jnp.arange(count, dtype=jnp.int32)[None, :] == target[:, None]
    sign = jnp.where(positive, jnp.float32(1.0), jnp.float32(-1.0))
    return (scale * (-sign * jax.nn.sigmoid(-sign * logits))).astype(jnp.bfloat16)


def per_device(images, texts, head, scale, bias, offsets):
    rows, width = images.shape
    share = head.shape[0]
    half = share // 2
    scale, bias, offset = scale[0], bias[0], offsets[0]
    core = lax.axis_index("core")

    text_a = lax.ppermute(texts, DP, by_chip(1))
    text_c = lax.ppermute(texts, DP, REST)
    text_b = lax.ppermute(text_a, "core", SWAP)

    own_half = lax.dynamic_slice_in_dim(head, core * half, half, 0)
    halves = spread(own_half, REP, 8)
    other = lax.ppermute(halves, "core", SWAP)
    full_head = jnp.where(
        core == 0, jnp.stack([halves, other], 1), jnp.stack([other, halves], 1)
    ).reshape(width, width)

    proj = dot(images, full_head, 1, 0)
    img_unit, inv_img = unit_rows(proj)
    img_b = img_unit.astype(jnp.bfloat16)
    txt_unit, inv_txt = unit_rows(texts.astype(jnp.float32))
    txt_b = txt_unit.astype(jnp.bfloat16)
    target = (jnp.arange(rows, dtype=jnp.int32) + offset) % rows

    img_dir = jnp.zeros((rows, width), jnp.float32)
    parts = []
    for index, block in enumerate((texts, text_a, text_b, text_c)):
        block_b = txt_b if index == 0 else unit_rows(block.astype(jnp.float32))[0].astype(jnp.bfloat16)
        weights = weights_of(img_b, block_b, scale, bias, target if index == 0 else None)
        img_dir = img_dir + dot(weights, block_b, 1, 0)
        parts.append(dot(weights, img_b, 0, 0))

    proj_grad = (
        (img_dir - img_unit * jnp.sum(img_unit * img_dir, axis=-1, keepdims=True)) * inv_img
    ).astype(jnp.bfloat16)

    from_b = lax.ppermute(parts[2].astype(jnp.bfloat16), "core", SWAP)
    back_c = lax.ppermute(parts[3].astype(jnp.bfloat16), DP, REST_BACK)
    pair = (parts[1] + from_b.astype(jnp.float32)).astype(jnp.bfloat16)
    back_a = lax.ppermute(pair, DP, by_chip(-1))

    term = dot(images, proj_grad, 0, 0).astype(jnp.bfloat16)
    term = term.reshape(8, 2, half, width).transpose(1, 0, 2, 3)
    term = exchange(term, "core")
    term = jnp.sum(term.astype(jnp.float32), axis=0).astype(jnp.bfloat16)
    term = exchange(term, REP)
    term = jnp.sum(term.astype(jnp.float32), axis=0).astype(jnp.bfloat16)
    padded = jnp.pad(term, ((0, 96 - half), (0, 0))).reshape(32, 3, width)
    padded = exchange(padded, RING)
    mine = jnp.sum(padded.astype(jnp.float32), axis=0).astype(jnp.bfloat16)
    done = spread(mine, RING, 32).reshape(96, width)[:half]
    head_grad = spread(done, "core", 2).reshape(share, width).astype(jnp.float32)

    image_grad = dot(proj_grad, full_head, 1, 1).astype(jnp.bfloat16)
    txt_dir = parts[0] + back_a.astype(jnp.float32) + back_c.astype(jnp.float32)
    text_grad = (
        (txt_dir - txt_unit * jnp.sum(txt_unit * txt_dir, axis=-1, keepdims=True)) * inv_txt
    ).astype(jnp.bfloat16)
    return image_grad, text_grad, head_grad


def solution(mesh):
    fine = Mesh(mesh.devices.reshape(8, 4, 2, 4, 2), ALL)
    in_specs = (P(ALL, None), P(ALL, None), P(REP, None), P(), P(), P(ALL))
    out_specs = (P(ALL, None), P(ALL, None), P(REP, None))
    return jax.shard_map(
        per_device, mesh=fine, in_specs=in_specs, out_specs=out_specs, check_vma=False
    )
```

```python
import jax
import jax.numpy as jnp
from jax import lax
from jax.sharding import Mesh
from jax.sharding import PartitionSpec as P

EPS = 1e-06
DP = ("z", "yh", "core")
RING = ("z", "yh")
REP = ("x", "yl")
ALL = DP + REP


def dot(a, b, ca, cb):
    return lax.dot_general(a, b, (((ca,), (cb,)), ((), ())), preferred_element_type=jnp.float32)


def by_chip(shift):
    return [(p, (p + 2 * shift) % 64) for p in range(64)]


SWAP = [(0, 1), (1, 0)]
AHEAD = [(p + 1, p) if p % 2 == 0 else ((p + 3) % 64, p) for p in range(64)]


def place(dp, x, y_lo):
    return dp * 8 + x * 2 + y_lo


def far_moves():
    first, second = [], []
    for x in range(4):
        for y_lo in range(2):
            for p in range(0, 64, 2):
                first.append((place(p, x, y_lo), place(p, x, y_lo)))
                second.append((place(p, x, y_lo), place(p + 1, x, y_lo)))
                source = (p + 61) % 64
                z, y, core = source // 8, (source // 2 % 4) * 2 + y_lo, source % 2
                back = (y + 7) % 8
                via = place((z * 4 + back // 2) * 2 + core, x, back % 2)
                first.append((place(source, x, y_lo), via))
                second.append((via, place(p, x, y_lo)))
    return sorted(first), sorted(second)


FAR_FIRST, FAR_SECOND = far_moves()


def exchange(array, axes):
    return lax.all_to_all(array, axes, split_axis=0, concat_axis=0, tiled=True)


def spread(array, axes, count):
    return exchange(jnp.broadcast_to(array[None], (count,) + array.shape), axes)


def unit_rows(values):
    inverse = lax.rsqrt(jnp.sum(values * values, axis=-1, keepdims=True) + EPS)
    return values * inverse, inverse


def negatives(logits, scale):
    return (scale * jax.nn.sigmoid(logits)).astype(jnp.bfloat16)


def off_unit(direction, unit, inverse):
    return (direction - unit * jnp.sum(unit * direction, axis=-1, keepdims=True)) * inverse


def per_device(images, texts, head, scale, bias, offsets):
    rows, width = images.shape
    share = head.shape[0]
    half = share // 2
    scale, bias, offset = scale[0], bias[0], offsets[0]
    core = lax.axis_index("core")

    far = lax.ppermute(texts, ALL, FAR_FIRST)
    text_a = lax.ppermute(texts, DP, by_chip(1))
    text_c = lax.ppermute(far, ALL, FAR_SECOND)
    text_b = lax.ppermute(text_a, "core", SWAP)

    own_half = lax.dynamic_slice_in_dim(head, core * half, half, 0)
    pair = spread(own_half, "yl", 2)
    halves = spread(pair, "x", 4)
    other = lax.ppermute(halves, "core", SWAP)
    halves, other = halves.reshape(8, half, width), other.reshape(8, half, width)
    full_head = jnp.where(
        core == 0, jnp.stack([halves, other], 1), jnp.stack([other, halves], 1)
    ).reshape(width, width)

    image_p = lax.ppermute(images, "core", SWAP)
    image_a = lax.ppermute(images, DP, by_chip(-1))
    image_c = lax.ppermute(images, DP, AHEAD)
    image_b = lax.ppermute(image_a, "core", SWAP)

    place_of = jnp.arange(width // 2, dtype=jnp.int32)
    wanted = (place_of // half) * share + core * half + place_of % half
    pick = (jnp.arange(width, dtype=jnp.int32)[:, None] == wanted[None, :]).astype(jnp.bfloat16)
    picked = jnp.concatenate([dot(images, pick, 1, 0), dot(image_p, pick, 1, 0)], 0).astype(jnp.bfloat16)

    proj = dot(images, full_head, 1, 0)
    img_unit, inv_img = unit_rows(proj)
    img_b = img_unit.astype(jnp.bfloat16)
    txt_unit, inv_txt = unit_rows(texts.astype(jnp.float32))
    txt_b = txt_unit.astype(jnp.bfloat16)
    target = (jnp.arange(rows, dtype=jnp.int32) + offset) % rows
    positive = jnp.arange(rows, dtype=jnp.int32)[None, :] == target[:, None]
    sign = jnp.where(positive, jnp.float32(1.0), jnp.float32(-1.0))
    logits = scale * dot(img_b, txt_b, 1, 1) + bias
    own_weights = (scale * (-sign * jax.nn.sigmoid(-sign * logits))).astype(jnp.bfloat16)

    img_dir = dot(own_weights, txt_b, 1, 0)
    for block in (text_a, text_b, text_c):
        block_b = unit_rows(block.astype(jnp.float32))[0].astype(jnp.bfloat16)
        weights = negatives(scale * dot(img_b, block_b, 1, 1) + bias, scale)
        img_dir = img_dir + dot(weights, block_b, 1, 0)
    proj_grad = off_unit(img_dir, img_unit, inv_img).astype(jnp.bfloat16)

    grad_p = lax.ppermute(proj_grad, "core", SWAP)
    term = dot(picked, jnp.concatenate([proj_grad, grad_p], 0), 0, 0).astype(jnp.bfloat16)
    term = exchange(term.reshape(8, half, width), REP)
    term = jnp.sum(term.astype(jnp.float32), axis=0).astype(jnp.bfloat16)
    padded = jnp.pad(term, ((0, 96 - half), (0, 0))).reshape(32, 3, width)
    padded = exchange(padded, RING)
    mine = jnp.sum(padded.astype(jnp.float32), axis=0).astype(jnp.bfloat16)
    done = spread(mine, RING, 32).reshape(96, width)[:half]
    head_grad = spread(done, "core", 2).reshape(share, width).astype(jnp.float32)

    image_grad = dot(proj_grad, full_head, 1, 1).astype(jnp.bfloat16)

    txt_dir = dot(own_weights, img_b, 0, 0)
    for block in (image_a, image_b, image_c):
        block_b = unit_rows(dot(block, full_head, 1, 0))[0].astype(jnp.bfloat16)
        weights = negatives(scale * dot(block_b, txt_b, 1, 1) + bias, scale)
        txt_dir = txt_dir + dot(weights, block_b, 0, 0)
    text_grad = off_unit(txt_dir, txt_unit, inv_txt).astype(jnp.bfloat16)
    return image_grad, text_grad, head_grad


def solution(mesh):
    fine = Mesh(mesh.devices.reshape(8, 4, 2, 4, 2), ALL)
    in_specs = (P(ALL, None), P(ALL, None), P(REP, None), P(), P(), P(ALL))
    out_specs = (P(ALL, None), P(ALL, None), P(REP, None))
    return jax.shard_map(
        per_device, mesh=fine, in_specs=in_specs, out_specs=out_specs, check_vma=False
    )
```

```python
import jax
import jax.numpy as jnp
from jax import lax
from jax.sharding import Mesh
from jax.sharding import PartitionSpec as P

EPS = 1e-06
DP = ("z", "yh", "core")
RING = ("z", "yh")
REP = ("x", "yl")
ALL = DP + REP


def dot(a, b, ca, cb):
    return lax.dot_general(a, b, (((ca,), (cb,)), ((), ())), preferred_element_type=jnp.float32)


def by_chip(shift):
    return [(p, (p + 2 * shift) % 64) for p in range(64)]


SWAP = [(0, 1), (1, 0)]
AHEAD = [(p + 1, p) if p % 2 == 0 else ((p + 3) % 64, p) for p in range(64)]


def place(dp, x, y_lo):
    return dp * 8 + x * 2 + y_lo


def far_moves():
    first, second = [], []
    for x in range(4):
        for y_lo in range(2):
            for p in range(0, 64, 2):
                first.append((place(p, x, y_lo), place(p, x, y_lo)))
                second.append((place(p, x, y_lo), place(p + 1, x, y_lo)))
                source = (p + 61) % 64
                z, y, core = source // 8, (source // 2 % 4) * 2 + y_lo, source % 2
                back = (y + 7) % 8
                via = place((z * 4 + back // 2) * 2 + core, x, back % 2)
                first.append((place(source, x, y_lo), via))
                second.append((via, place(p, x, y_lo)))
    return sorted(first), sorted(second)


FAR_FIRST, FAR_SECOND = far_moves()


def exchange(array, axes):
    return lax.all_to_all(array, axes, split_axis=0, concat_axis=0, tiled=True)


def spread(array, axes, count):
    return exchange(jnp.broadcast_to(array[None], (count,) + array.shape), axes)


def unit_rows(values):
    inverse = lax.rsqrt(jnp.sum(values * values, axis=-1, keepdims=True) + EPS)
    return values * inverse, inverse


def negatives(logits, scale):
    return (scale * jax.nn.sigmoid(logits)).astype(jnp.bfloat16)


def off_unit(direction, unit, inverse):
    return (direction - unit * jnp.sum(unit * direction, axis=-1, keepdims=True)) * inverse


def per_device(images, texts, head, scale, bias, offsets):
    rows, width = images.shape
    share = head.shape[0]
    half = share // 2
    scale, bias, offset = scale[0], bias[0], offsets[0]
    core = lax.axis_index("core")

    far = lax.ppermute(texts, ALL, FAR_FIRST)
    text_a = lax.ppermute(texts, DP, by_chip(1))
    text_c = lax.ppermute(far, ALL, FAR_SECOND)
    text_b = lax.ppermute(text_a, "core", SWAP)

    own_half = lax.dynamic_slice_in_dim(head, core * half, half, 0)
    across = lax.ppermute(own_half, "yl", SWAP)
    pair = jnp.where(
        lax.axis_index("yl") == 0, jnp.stack([own_half, across]), jnp.stack([across, own_half])
    )
    halves = spread(pair, "x", 4)
    other = lax.ppermute(halves, "core", SWAP)
    halves, other = halves.reshape(8, half, width), other.reshape(8, half, width)
    full_head = jnp.where(
        core == 0, jnp.stack([halves, other], 1), jnp.stack([other, halves], 1)
    ).reshape(width, width)

    image_p = lax.ppermute(images, "core", SWAP)
    later = images + text_a[0, 0] * 0
    image_a = lax.ppermute(later, DP, by_chip(-1))
    image_c = lax.ppermute(later, DP, AHEAD)
    image_b = lax.ppermute(image_a, "core", SWAP)

    place_of = jnp.arange(width // 2, dtype=jnp.int32)
    wanted = (place_of // half) * share + core * half + place_of % half
    pick = (jnp.arange(width, dtype=jnp.int32)[:, None] == wanted[None, :]).astype(jnp.bfloat16)
    picked = jnp.concatenate([dot(images, pick, 1, 0), dot(image_p, pick, 1, 0)], 0).astype(jnp.bfloat16)

    proj = dot(images, full_head, 1, 0)
    img_unit, inv_img = unit_rows(proj)
    img_b = img_unit.astype(jnp.bfloat16)
    txt_unit, inv_txt = unit_rows(texts.astype(jnp.float32))
    txt_b = txt_unit.astype(jnp.bfloat16)
    target = (jnp.arange(rows, dtype=jnp.int32) + offset) % rows
    positive = jnp.arange(rows, dtype=jnp.int32)[None, :] == target[:, None]
    sign = jnp.where(positive, jnp.float32(1.0), jnp.float32(-1.0))
    logits = scale * dot(img_b, txt_b, 1, 1) + bias
    own_weights = (scale * (-sign * jax.nn.sigmoid(-sign * logits))).astype(jnp.bfloat16)

    img_dir = dot(own_weights, txt_b, 1, 0)
    for block in (text_a, text_b, text_c):
        block_b = unit_rows(block.astype(jnp.float32))[0].astype(jnp.bfloat16)
        weights = negatives(scale * dot(img_b, block_b, 1, 1) + bias, scale)
        img_dir = img_dir + dot(weights, block_b, 1, 0)
    proj_grad = off_unit(img_dir, img_unit, inv_img).astype(jnp.bfloat16)

    grad_p = lax.ppermute(proj_grad, "core", SWAP)
    term = dot(picked, jnp.concatenate([proj_grad, grad_p], 0), 0, 0).astype(jnp.bfloat16)
    term = exchange(term.reshape(8, half, width), REP)
    term = jnp.sum(term.astype(jnp.float32), axis=0).astype(jnp.bfloat16)
    padded = jnp.pad(term, ((0, 96 - half), (0, 0))).reshape(32, 3, width)
    padded = exchange(padded, RING)
    mine = jnp.sum(padded.astype(jnp.float32), axis=0).astype(jnp.bfloat16)
    done = spread(mine, RING, 32).reshape(96, width)[:half]
    head_grad = spread(done, "core", 2).reshape(share, width).astype(jnp.float32)

    image_grad = dot(proj_grad, full_head, 1, 1).astype(jnp.bfloat16)

    txt_dir = dot(own_weights, img_b, 0, 0)
    for block in (image_a, image_b, image_c):
        block_b = unit_rows(dot(block, full_head, 1, 0))[0].astype(jnp.bfloat16)
        weights = negatives(scale * dot(block_b, txt_b, 1, 1) + bias, scale)
        txt_dir = txt_dir + dot(weights, block_b, 0, 0)
    text_grad = off_unit(txt_dir, txt_unit, inv_txt).astype(jnp.bfloat16)
    return image_grad, text_grad, head_grad


def solution(mesh):
    fine = Mesh(mesh.devices.reshape(8, 4, 2, 4, 2), ALL)
    in_specs = (P(ALL, None), P(ALL, None), P(REP, None), P(), P(), P(ALL))
    out_specs = (P(ALL, None), P(ALL, None), P(REP, None))
    return jax.shard_map(
        per_device, mesh=fine, in_specs=in_specs, out_specs=out_specs, check_vma=False
    )
```

```python
import jax
import jax.numpy as jnp
from jax import lax
from jax.experimental import pallas as pl
from jax.experimental.pallas import tpu as pltpu
from jax.sharding import Mesh
from jax.sharding import PartitionSpec as P

EPS = 1e-06
CHAIN = 20_000_000_000
DP = ("z", "yh", "core")
RING = ("z", "yh")
REP = ("x", "yl")
ALL = DP + REP


def dot(a, b, ca, cb):
    return lax.dot_general(a, b, (((ca,), (cb,)), ((), ())), preferred_element_type=jnp.float32)


def by_chip(shift):
    return [(p, (p + 2 * shift) % 64) for p in range(64)]


SWAP = [(0, 1), (1, 0)]
ON = [(p, (p + 1) % 64) for p in range(64)]
BACK = [(b, a) for a, b in ON]


def exchange(array, axes):
    return lax.all_to_all(array, axes, split_axis=0, concat_axis=0, tiled=True)


def spread(array, axes, count):
    return exchange(jnp.broadcast_to(array[None], (count,) + array.shape), axes)


def unit_rows(values):
    inverse = lax.rsqrt(jnp.sum(values * values, axis=-1, keepdims=True) + EPS)
    return values * inverse, inverse


def off_unit(direction, unit, inverse):
    return (direction - unit * jnp.sum(unit * direction, axis=-1, keepdims=True)) * inverse


def narrow(values):
    return values.astype(jnp.bfloat16)


def rounded_unit(block):
    return narrow(unit_rows(block.astype(jnp.float32))[0])


def negatives(a, b, numbers):
    logits = numbers[0] * dot(a, b, 1, 1) + numbers[1]
    return narrow(numbers[0] * jax.nn.sigmoid(logits))


def own_pairs(a, b, numbers, positive):
    logits = numbers[0] * dot(a, b, 1, 1) + numbers[1]
    sign = jnp.where(positive, jnp.float32(1.0), jnp.float32(-1.0))
    return narrow(numbers[0] * (-sign * jax.nn.sigmoid(-sign * logits)))


def positives(offset, rows, image_dim):
    image = lax.broadcasted_iota(jnp.int32, (rows, rows), image_dim)
    text = lax.broadcasted_iota(jnp.int32, (rows, rows), 1 - image_dim)
    target = image + offset
    return text == jnp.where(target >= rows, target - rows, target)


def image_kernel(numbers, offset, images, head, texts, text_a, text_b, here, unit, inverse, img_b, partial):
    proj = dot(images[...], head[...], 1, 0)
    unit_value, inverse_value = unit_rows(proj)
    unit[...] = unit_value
    inverse[...] = jnp.broadcast_to(inverse_value, inverse.shape)
    rounded = narrow(unit_value)
    img_b[...] = rounded
    block = rounded_unit(texts[...])
    weights = own_pairs(rounded, block, numbers, positives(offset[0], block.shape[0], 0))
    total = dot(weights, block, 1, 0)
    for other in (text_a, text_b):
        block = rounded_unit(other[...])
        total = total + dot(negatives(rounded, block, numbers), block, 1, 0)
    partial[...] = total


def last_kernel(numbers, text_c, unit, inverse, img_b, partial, here, picked, proj_grad):
    block = rounded_unit(text_c[...])
    total = partial[...] + dot(negatives(img_b[...], block, numbers), block, 1, 0)
    proj_grad[...] = narrow(off_unit(total, unit[...], inverse[:, :1]))


def text_kernel(numbers, offset, texts, img_b, head, image_a, image_b, image_c, text_grad):
    unit, inverse = unit_rows(texts[...].astype(jnp.float32))
    txt_b = narrow(unit)
    own = img_b[...]
    weights = own_pairs(txt_b, own, numbers, positives(offset[0], own.shape[0], 1))
    total = dot(weights, own, 1, 0)
    for other in (image_a, image_b, image_c):
        block = narrow(unit_rows(dot(other[...], head[...], 1, 0))[0])
        total = total + dot(negatives(txt_b, block, numbers), block, 1, 0)
    text_grad[...] = narrow(off_unit(total, unit, inverse))


def choose_kernel(which, first, second, out):
    out[...] = jnp.where(which[0] == 0, first[...], second[...])


def pick_kernel(core, images, image_p, picked):
    half, width = picked.shape[0] // 8, images.shape[1]
    row = lax.broadcasted_iota(jnp.int32, (picked.shape[0], width), 0)
    column = lax.broadcasted_iota(jnp.int32, (picked.shape[0], width), 1)
    wanted = row + (row // half + core[0]) * half
    pick = jnp.where(column == wanted, jnp.float32(1.0), jnp.float32(0.0)).astype(jnp.bfloat16)
    count = images.shape[0]
    picked[:, :count] = narrow(dot(pick, images[...], 1, 1))
    picked[:, count:] = narrow(dot(pick, image_p[...], 1, 1))


def term_kernel(picked, grad, grad_p, out):
    count, half = grad.shape[0], out.shape[1]
    term = dot(picked[:, :count], grad[...], 1, 0) + dot(picked[:, count:], grad_p[...], 1, 0)
    for index in range(out.shape[0]):
        out[index] = narrow(term[index * half : (index + 1) * half])


def group_kernel(term, here, out):
    total = term[0].astype(jnp.float32)
    for index in range(1, term.shape[0]):
        total = total + term[index].astype(jnp.float32)
    rows, third = out.shape[1:]
    groups = total.shape[0] // rows
    for group in range(groups):
        for part in range(3):
            piece = total[group * rows : (group + 1) * rows, part * third : (part + 1) * third]
            out[group * 3 + part] = narrow(piece)
    for index in range(groups * 3, out.shape[0]):
        out[index] = jnp.zeros((rows, third), out.dtype)


def copies_kernel(pieces, here, out):
    total = pieces[0].astype(jnp.float32)
    for index in range(1, pieces.shape[0]):
        total = total + pieces[index].astype(jnp.float32)
    for index in range(out.shape[0]):
        out[index] = narrow(total)


def join_kernel(pieces, out):
    rows, third = pieces.shape[1:]
    groups = out.shape[1] // rows
    total = jnp.concatenate(
        [
            jnp.concatenate([pieces[g * 3 + p].astype(jnp.float32) for p in range(3)], 1)
            for g in range(groups)
        ],
        0,
    )
    for index in range(out.shape[0]):
        out[index] = narrow(total)


def call(kernel, scalars, arrays, outs, flops, after=()):
    smem, vmem = pl.BlockSpec(memory_space=pltpu.SMEM), pl.BlockSpec(memory_space=pltpu.VMEM)
    moved = sum(a.size * a.dtype.itemsize for a in list(arrays) + list(outs))
    return pl.pallas_call(
        kernel,
        out_shape=outs if len(outs) > 1 else outs[0],
        in_specs=[smem] * len(scalars) + [vmem] * len(arrays) + [pl.BlockSpec(memory_space=pl.ANY)] * len(after),
        out_specs=[vmem] * len(outs) if len(outs) > 1 else vmem,
        compiler_params=pltpu.CompilerParams(vmem_limit_bytes=40 * 1024 * 1024),
        cost_estimate=pl.CostEstimate(flops=flops, bytes_accessed=moved, transcendentals=0),
    )(*scalars, *arrays, *after)


def per_device(images, texts, head, scale, bias, offsets):
    rows, width = images.shape
    share = head.shape[0]
    half = share // 2
    core = lax.axis_index("core")
    numbers = jnp.concatenate([scale, bias])
    pair_flops = 4 * rows * rows * width
    full_flops = 2 * rows * width * width
    wide = jax.ShapeDtypeStruct((rows, width), jnp.float32)
    slim = jax.ShapeDtypeStruct((rows, width), jnp.bfloat16)

    text_a = lax.ppermute(texts, DP, by_chip(1))
    image_a = lax.ppermute(images, DP, by_chip(-1))
    text_b = lax.ppermute(text_a, "core", SWAP)
    image_b = lax.ppermute(image_a, "core", SWAP)
    mine = lax.convert_element_type(core, jnp.int32).reshape(1)
    text_on = call(choose_kernel, (mine,), (texts, text_a), (slim,), CHAIN)
    image_on = call(choose_kernel, (1 - mine,), (images, image_a), (slim,), CHAIN)
    text_c = lax.ppermute(text_on, DP, ON)
    image_c = lax.ppermute(image_on, DP, BACK)

    own_half = lax.dynamic_slice_in_dim(head, core * half, half, 0)
    across = lax.ppermute(own_half, "yl", SWAP)
    pair = jnp.where(
        lax.axis_index("yl") == 0, jnp.stack([own_half, across]), jnp.stack([across, own_half])
    )
    halves = spread(pair, "x", 4)
    other = lax.ppermute(halves, "core", SWAP)
    halves, other = halves.reshape(8, half, width), other.reshape(8, half, width)
    full_head = jnp.where(
        core == 0, jnp.stack([halves, other], 1), jnp.stack([other, halves], 1)
    ).reshape(width, width)

    image_p = lax.ppermute(images, "core", SWAP)
    picked = call(
        pick_kernel,
        (mine,),
        (images, image_p),
        (jax.ShapeDtypeStruct((width // 2, 2 * rows), jnp.bfloat16),),
        2 * full_flops,
    )
    unit, inverse, img_b, partial = call(
        image_kernel,
        (numbers, offsets),
        (images, full_head, texts, text_a, text_b),
        (wide, jax.ShapeDtypeStruct((rows, 128), jnp.float32), slim, wide),
        full_flops + 3 * pair_flops,
        (image_a,),
    )
    proj_grad = call(
        last_kernel, (numbers,), (text_c, unit, inverse, img_b, partial), (slim,), pair_flops, (image_c, picked)
    )

    grad_p = lax.ppermute(proj_grad, "core", SWAP)
    pieces = jax.ShapeDtypeStruct((32, 8, width // 3), jnp.bfloat16)
    term = call(
        term_kernel,
        (),
        (picked, proj_grad, grad_p),
        (jax.ShapeDtypeStruct((8, half, width), jnp.bfloat16),),
        full_flops,
    )
    term = exchange(term, REP)
    text_grad = call(
        text_kernel,
        (numbers, offsets),
        (texts, img_b, full_head, image_a, image_b, image_c),
        (slim,),
        3 * full_flops + 4 * pair_flops,
    )
    term = call(group_kernel, (), (term,), (pieces,), term.size, (text_grad,))
    term = exchange(term, RING)
    image_grad = dot(proj_grad, full_head, 1, 1).astype(jnp.bfloat16)
    copies = call(copies_kernel, (), (term,), (pieces,), term.size, (image_grad,))
    done = exchange(copies, RING)
    done = call(
        join_kernel, (), (done,), (jax.ShapeDtypeStruct((2, half, width), jnp.bfloat16),), done.size
    )
    head_grad = exchange(done, "core").reshape(share, width).astype(jnp.float32)
    return image_grad, text_grad, head_grad


def solution(mesh):
    fine = Mesh(mesh.devices.reshape(8, 4, 2, 4, 2), ALL)
    in_specs = (P(ALL, None), P(ALL, None), P(REP, None), P(), P(), P(ALL))
    out_specs = (P(ALL, None), P(ALL, None), P(REP, None))
    return jax.shard_map(
        per_device, mesh=fine, in_specs=in_specs, out_specs=out_specs, check_vma=False
    )
```

```python
import jax
import jax.numpy as jnp
from jax import lax
from jax.experimental import pallas as pl
from jax.experimental.pallas import tpu as pltpu
from jax.sharding import Mesh
from jax.sharding import PartitionSpec as P

EPS = 1e-06
CHAIN = 20_000_000_000
DP = ("z", "yh", "core")
RING = ("z", "yh")
REP = ("x", "yl")
ALL = DP + REP


def dot(a, b, ca, cb):
    return lax.dot_general(a, b, (((ca,), (cb,)), ((), ())), preferred_element_type=jnp.float32)


def by_chip(shift):
    return [(p, (p + 2 * shift) % 64) for p in range(64)]


SWAP = [(0, 1), (1, 0)]
CROSS = [(0, 1), (3, 2)]
FAR = [(p, (p + (1 if p % 2 else 63)) % 64) for p in range(64)]


def exchange(array, axes):
    return lax.all_to_all(array, axes, split_axis=0, concat_axis=0, tiled=True)


def unit_rows(values):
    inverse = lax.rsqrt(jnp.sum(values * values, axis=-1, keepdims=True) + EPS)
    return values * inverse, inverse


def off_unit(direction, unit, inverse):
    return (direction - unit * jnp.sum(unit * direction, axis=-1, keepdims=True)) * inverse


def narrow(values):
    return values.astype(jnp.bfloat16)


def rounded_unit(block):
    return narrow(unit_rows(block.astype(jnp.float32))[0])


def negatives(a, b, numbers):
    logits = numbers[0] * dot(a, b, 1, 1) + numbers[1]
    return narrow(numbers[0] * jax.nn.sigmoid(logits))


def own_pairs(a, b, numbers, positive):
    logits = numbers[0] * dot(a, b, 1, 1) + numbers[1]
    sign = jnp.where(positive, jnp.float32(1.0), jnp.float32(-1.0))
    return narrow(numbers[0] * (-sign * jax.nn.sigmoid(-sign * logits)))


def positives(offset, rows, image_dim):
    image = lax.broadcasted_iota(jnp.int32, (rows, rows), image_dim)
    text = lax.broadcasted_iota(jnp.int32, (rows, rows), 1 - image_dim)
    target = image + offset
    return text == jnp.where(target >= rows, target - rows, target)


def head_kernel(crossed, head, across, copies):
    shard = jnp.where(crossed[0] == 1, across[...], head[...])
    for index in range(copies.shape[0]):
        copies[index] = shard


def turn_kernel(core, texts, text_a, image_a, units, onward):
    rows = texts.shape[0]
    units[:rows] = rounded_unit(text_a[...])
    units[rows:] = rounded_unit(texts[...])
    onward[...] = jnp.where(core[0] == 0, image_a[...], text_a[...])


def stack_kernel(first, second, out):
    rows = first.shape[0]
    out[:rows] = first[...]
    out[rows:] = second[...]


def first_kernel(
    numbers, offset, core, pair, halves, other, units,
    head, unit, inverse, img_b, far_unit, far_inverse, far_b, partial,
):
    count, share = halves.shape[:2]
    for index in range(count):
        for source, place in ((halves, core[0]), (other, 1 - core[0])):
            start = pl.multiple_of((2 * index + place) * share, 16)
            head[pl.ds(start, share), :] = source[index]

    rows = img_b.shape[0]
    unit_value, inverse_value = unit_rows(dot(pair[rows:], head[...], 1, 0))
    unit[...] = unit_value
    inverse[...] = jnp.broadcast_to(inverse_value, inverse.shape)
    rounded = narrow(unit_value)
    img_b[...] = rounded

    @pl.when(core[0] == 0)
    def _():
        unit_value, inverse_value = unit_rows(dot(pair[:rows], head[...], 1, 0))
        far_unit[...] = unit_value
        far_inverse[...] = jnp.broadcast_to(inverse_value, far_inverse.shape)
        far_b[...] = narrow(unit_value)

    @pl.when(core[0] != 0)
    def _():
        far_unit[...] = unit[...]
        far_inverse[...] = inverse[...]
        far_b[...] = img_b[...]

    block = units[rows:]
    weights = own_pairs(rounded, block, numbers, positives(offset[0], rows, 0))
    total = dot(weights, block, 1, 0)
    block = units[:rows]
    partial[...] = total + dot(negatives(rounded, block, numbers), block, 1, 0)


def grad_kernel(
    numbers, core, units_p, unit, inverse, img_b, far_unit, far_inverse, far_b, partial, here,
    grads,
):
    rows = img_b.shape[0]
    block = units_p[:rows]
    total = partial[...] + dot(negatives(img_b[...], block, numbers), block, 1, 0)
    grad = off_unit(total, unit[...], inverse[:, :1])
    far = jnp.where(core[0] == 0, block, units_p[rows:])
    total = dot(negatives(far_b[...], far, numbers), far, 1, 0)
    far_grad = off_unit(total, far_unit[...], far_inverse[:, :1])

    @pl.when(core[0] == 0)
    def _():
        grads[:rows] = narrow(grad)
        grads[rows:] = narrow(far_grad)

    @pl.when(core[0] != 0)
    def _():
        grads[:rows] = narrow(grad + far_grad)
        grads[rows:] = jnp.zeros_like(far_grad, grads.dtype)


def text_kernel(numbers, offset, core, texts, img_b, head, image_a, pair_p, far, text_grad):
    unit, inverse = unit_rows(texts[...].astype(jnp.float32))
    txt_b = narrow(unit)
    own = img_b[...]
    weights = own_pairs(txt_b, own, numbers, positives(offset[0], own.shape[0], 1))
    total = dot(weights, own, 1, 0)
    rows = own.shape[0]
    last = jnp.where(core[0] == 0, pair_p[rows:], far[...])
    for other in (image_a[...], pair_p[:rows], last):
        block = narrow(unit_rows(dot(other, head[...], 1, 0))[0])
        total = total + dot(negatives(txt_b, block, numbers), block, 1, 0)
    text_grad[...] = narrow(off_unit(total, unit, inverse))


def image_grad_kernel(numbers, core, grads, far, unit, inverse, img_b, head, image_grad):
    block = rounded_unit(far[...])
    total = dot(negatives(img_b[...], block, numbers), block, 1, 0)
    extra = jnp.where(core[0] == 0, off_unit(total, unit[...], inverse[:, :1]), jnp.float32(0.0))
    grad = narrow(grads[: block.shape[0]].astype(jnp.float32) + extra)
    image_grad[...] = narrow(dot(grad, head[...], 1, 1))


def pick_kernel(core, pair, pair_p, picked):
    half, width = picked.shape[0] // 8, pair.shape[1]
    row = lax.broadcasted_iota(jnp.int32, (picked.shape[0], width), 0)
    column = lax.broadcasted_iota(jnp.int32, (picked.shape[0], width), 1)
    wanted = row + (row // half + core[0]) * half
    pick = jnp.where(column == wanted, jnp.float32(1.0), jnp.float32(0.0)).astype(jnp.bfloat16)
    count = pair.shape[0] // 2
    far = jnp.where(core[0] == 0, pair[:count], pair_p[:count])
    for index, block in enumerate((pair[count:], pair_p[count:], far)):
        picked[:, index * count : (index + 1) * count] = narrow(dot(pick, block, 1, 1))


def near_term_kernel(core, picked, grads, here, total):
    count = grads.shape[0] // 2
    total[...] = dot(picked[:, :count], grads[:count], 1, 0)


def term_kernel(core, picked, grads, grads_p, total, out):
    count, half = grads.shape[0] // 2, out.shape[1]
    far = jnp.where(core[0] == 0, grads[count:], grads_p[count:])
    term = total[...] + dot(picked[:, count : 2 * count], grads_p[:count], 1, 0)
    term = term + dot(picked[:, 2 * count :], far, 1, 0)
    for index in range(out.shape[0]):
        out[index] = narrow(term[index * half : (index + 1) * half])


def group_kernel(term, here, out):
    total = term[0].astype(jnp.float32)
    for index in range(1, term.shape[0]):
        total = total + term[index].astype(jnp.float32)
    rows, third = out.shape[1:]
    groups = total.shape[0] // rows
    for group in range(groups):
        for part in range(3):
            piece = total[group * rows : (group + 1) * rows, part * third : (part + 1) * third]
            out[group * 3 + part] = narrow(piece)
    for index in range(groups * 3, out.shape[0]):
        out[index] = jnp.zeros((rows, third), out.dtype)


def copies_kernel(pieces, here, out):
    total = pieces[0].astype(jnp.float32)
    for index in range(1, pieces.shape[0]):
        total = total + pieces[index].astype(jnp.float32)
    for index in range(out.shape[0]):
        out[index] = narrow(total)


def join_kernel(pieces, out):
    rows, third = pieces.shape[1:]
    groups = out.shape[1] // rows
    total = jnp.concatenate(
        [
            jnp.concatenate([pieces[g * 3 + p].astype(jnp.float32) for p in range(3)], 1)
            for g in range(groups)
        ],
        0,
    )
    for index in range(out.shape[0]):
        out[index] = narrow(total)


def call(kernel, scalars, arrays, outs, flops, after=()):
    smem, vmem = pl.BlockSpec(memory_space=pltpu.SMEM), pl.BlockSpec(memory_space=pltpu.VMEM)
    moved = sum(a.size * a.dtype.itemsize for a in list(arrays) + list(outs))
    return pl.pallas_call(
        kernel,
        out_shape=outs if len(outs) > 1 else outs[0],
        in_specs=[smem] * len(scalars) + [vmem] * len(arrays) + [pl.BlockSpec(memory_space=pl.ANY)] * len(after),
        out_specs=[vmem] * len(outs) if len(outs) > 1 else vmem,
        compiler_params=pltpu.CompilerParams(vmem_limit_bytes=24 * 1024 * 1024),
        cost_estimate=pl.CostEstimate(flops=flops, bytes_accessed=moved, transcendentals=0),
    )(*scalars, *arrays, *after)


def per_device(images, texts, head, scale, bias, offsets):
    rows, width = images.shape
    share = head.shape[0]
    half = share // 2
    core = lax.axis_index("core")
    numbers = jnp.concatenate([scale, bias])
    pair_flops = 4 * rows * rows * width
    full_flops = 2 * rows * width * width
    wide = jax.ShapeDtypeStruct((rows, width), jnp.float32)
    slim = jax.ShapeDtypeStruct((rows, width), jnp.bfloat16)

    mine = lax.convert_element_type(core, jnp.int32).reshape(1)
    text_a = lax.ppermute(texts, DP, by_chip(1))
    image_a = lax.ppermute(images, DP, by_chip(-1))
    twice = jax.ShapeDtypeStruct((2 * rows, width), jnp.bfloat16)
    image_pair = call(stack_kernel, (), (image_a, images), (twice,), rows)
    image_pair_p = lax.ppermute(image_pair, "core", SWAP)
    units, onward = call(turn_kernel, (mine,), (texts, text_a, image_a), (twice, slim), CHAIN)
    units_p = lax.ppermute(units, "core", SWAP)
    far = lax.ppermute(onward, DP, FAR)

    y_lo = lax.axis_index("yl")
    across = lax.ppermute(head, ("core", "yl"), CROSS)
    crossed = lax.convert_element_type(core != y_lo, jnp.int32).reshape(1)
    copies = call(
        head_kernel,
        (crossed,),
        (head, across),
        (jax.ShapeDtypeStruct((4, share, width), jnp.bfloat16),),
        2 * CHAIN,
    )
    halves = exchange(copies, "x")
    other = lax.ppermute(halves, "core", SWAP)

    picked = call(
        pick_kernel,
        (mine,),
        (image_pair, image_pair_p),
        (jax.ShapeDtypeStruct((width // 2, 3 * rows), jnp.bfloat16),),
        CHAIN,
    )
    slight = jax.ShapeDtypeStruct((rows, 128), jnp.float32)
    full_head, unit, inverse, img_b, far_unit, far_inverse, far_b, partial = call(
        first_kernel,
        (numbers, offsets, mine),
        (image_pair, halves, other, units),
        (jax.ShapeDtypeStruct((width, width), jnp.bfloat16), wide, slight, slim, wide, slight, slim, wide),
        CHAIN,
    )
    grads = call(
        grad_kernel,
        (numbers, mine),
        (units_p, unit, inverse, img_b, far_unit, far_inverse, far_b, partial),
        (jax.ShapeDtypeStruct((2 * rows, width), jnp.bfloat16),),
        rows,
        (picked,),
    )

    grads_p = lax.ppermute(grads, "core", SWAP)
    pieces = jax.ShapeDtypeStruct((32, 8, width // 3), jnp.bfloat16)
    near = call(
        near_term_kernel,
        (mine,),
        (picked, grads),
        (jax.ShapeDtypeStruct((width // 2, width), jnp.float32),),
        CHAIN // 2,
        (far,),
    )
    term = call(
        term_kernel,
        (mine,),
        (picked, grads, grads_p, near),
        (jax.ShapeDtypeStruct((8, half, width), jnp.bfloat16),),
        full_flops,
    )
    term = exchange(term, REP)
    text_grad = call(
        text_kernel,
        (numbers, offsets, mine),
        (texts, img_b, full_head, image_a, image_pair_p, far),
        (slim,),
        3 * full_flops + 4 * pair_flops,
    )
    term = call(group_kernel, (), (term,), (pieces,), term.size, (text_grad,))
    term = exchange(term, RING)
    image_grad = call(
        image_grad_kernel,
        (numbers, mine),
        (grads, far, unit, inverse, img_b, full_head),
        (slim,),
        full_flops + pair_flops,
    )
    copies = call(copies_kernel, (), (term,), (pieces,), term.size, (image_grad,))
    done = exchange(copies, RING)
    done = call(
        join_kernel, (), (done,), (jax.ShapeDtypeStruct((2, half, width), jnp.bfloat16),), done.size
    )
    head_grad = exchange(done, "core").reshape(share, width).astype(jnp.float32)
    return image_grad, text_grad, head_grad


def solution(mesh):
    fine = Mesh(mesh.devices.reshape(8, 4, 2, 4, 2), ALL)
    in_specs = (P(ALL, None), P(ALL, None), P(REP, None), P(), P(), P(ALL))
    out_specs = (P(ALL, None), P(ALL, None), P(REP, None))
    return jax.shard_map(
        per_device, mesh=fine, in_specs=in_specs, out_specs=out_specs, check_vma=False
    )
```

```python
import jax
import jax.numpy as jnp
from jax import lax
from jax.experimental import pallas as pl
from jax.experimental.pallas import tpu as pltpu
from jax.sharding import Mesh
from jax.sharding import PartitionSpec as P

EPS = 1e-06
CHAIN = 20_000_000_000
DP = ("z", "yh", "core")
RING = ("z", "yh")
REP = ("x", "yl")
ALL = DP + REP


def dot(a, b, ca, cb):
    return lax.dot_general(a, b, (((ca,), (cb,)), ((), ())), preferred_element_type=jnp.float32)


def by_chip(shift):
    return [(p, (p + 2 * shift) % 64) for p in range(64)]


SWAP = [(0, 1), (1, 0)]
CROSS = [(0, 1), (3, 2)]
FAR = [(p, (p + (1 if p % 2 else 63)) % 64) for p in range(64)]


def exchange(array, axes):
    return lax.all_to_all(array, axes, split_axis=0, concat_axis=0, tiled=True)


def unit_rows(values):
    inverse = lax.rsqrt(jnp.sum(values * values, axis=-1, keepdims=True) + EPS)
    return values * inverse, inverse


def off_unit(direction, unit, inverse):
    return (direction - unit * jnp.sum(unit * direction, axis=-1, keepdims=True)) * inverse


def narrow(values):
    return values.astype(jnp.bfloat16)


def rounded_unit(block):
    return narrow(unit_rows(block.astype(jnp.float32))[0])


def negatives(a, b, numbers):
    logits = numbers[0] * dot(a, b, 1, 1) + numbers[1]
    return narrow(numbers[0] * jax.nn.sigmoid(logits))


def own_pairs(a, b, numbers, positive):
    logits = numbers[0] * dot(a, b, 1, 1) + numbers[1]
    sign = jnp.where(positive, jnp.float32(1.0), jnp.float32(-1.0))
    return narrow(numbers[0] * (-sign * jax.nn.sigmoid(-sign * logits)))


def positives(offset, rows, image_dim):
    image = lax.broadcasted_iota(jnp.int32, (rows, rows), image_dim)
    text = lax.broadcasted_iota(jnp.int32, (rows, rows), 1 - image_dim)
    target = image + offset
    return text == jnp.where(target >= rows, target - rows, target)


def head_kernel(crossed, head, across, copies):
    shard = jnp.where(crossed[0] == 1, across[...], head[...])
    for index in range(copies.shape[0]):
        copies[index] = shard


def turn_kernel(core, texts, text_a, image_a, units, onward):
    rows = texts.shape[0]
    units[:rows] = rounded_unit(text_a[...])
    units[rows:] = rounded_unit(texts[...])
    onward[...] = jnp.where(core[0] == 0, image_a[...], text_a[...])


def stack_kernel(first, second, out):
    rows = first.shape[0]
    out[:rows] = first[...]
    out[rows:] = second[...]


def first_kernel(
    numbers, offset, core, pair, halves, other, units,
    head, unit, inverse, img_b, far_unit, far_inverse, far_b, partial,
):
    count, share = halves.shape[:2]
    for index in range(count):
        for source, place in ((halves, core[0]), (other, 1 - core[0])):
            start = pl.multiple_of((2 * index + place) * share, 16)
            head[pl.ds(start, share), :] = source[index]

    rows = img_b.shape[0]
    unit_value, inverse_value = unit_rows(dot(pair[rows:], head[...], 1, 0))
    unit[...] = unit_value
    inverse[...] = jnp.broadcast_to(inverse_value, inverse.shape)
    rounded = narrow(unit_value)
    img_b[...] = rounded

    @pl.when(core[0] == 0)
    def _():
        unit_value, inverse_value = unit_rows(dot(pair[:rows], head[...], 1, 0))
        far_unit[...] = unit_value
        far_inverse[...] = jnp.broadcast_to(inverse_value, far_inverse.shape)
        far_b[...] = narrow(unit_value)

    @pl.when(core[0] != 0)
    def _():
        far_unit[...] = unit[...]
        far_inverse[...] = inverse[...]
        far_b[...] = img_b[...]

    block = units[rows:]
    weights = own_pairs(rounded, block, numbers, positives(offset[0], rows, 0))
    total = dot(weights, block, 1, 0)
    block = units[:rows]
    partial[...] = total + dot(negatives(rounded, block, numbers), block, 1, 0)


def grad_kernel(
    numbers, core, units_p, unit, inverse, img_b, far_unit, far_inverse, far_b, partial, here,
    grads,
):
    rows = img_b.shape[0]
    block = units_p[:rows]
    total = partial[...] + dot(negatives(img_b[...], block, numbers), block, 1, 0)
    grad = off_unit(total, unit[...], inverse[:, :1])
    far = jnp.where(core[0] == 0, block, units_p[rows:])
    total = dot(negatives(far_b[...], far, numbers), far, 1, 0)
    far_grad = off_unit(total, far_unit[...], far_inverse[:, :1])

    @pl.when(core[0] == 0)
    def _():
        grads[:rows] = narrow(grad)
        grads[rows:] = narrow(far_grad)

    @pl.when(core[0] != 0)
    def _():
        grads[:rows] = narrow(grad + far_grad)
        grads[rows:] = jnp.zeros_like(far_grad, grads.dtype)


def text_kernel(numbers, offset, core, texts, img_b, head, image_a, pair_p, far, text_grad, token):
    unit, inverse = unit_rows(texts[...].astype(jnp.float32))
    txt_b = narrow(unit)
    own = img_b[...]
    weights = own_pairs(txt_b, own, numbers, positives(offset[0], own.shape[0], 1))
    total = dot(weights, own, 1, 0)
    rows = own.shape[0]
    last = jnp.where(core[0] == 0, pair_p[rows:], far[...])
    for other in (image_a[...], pair_p[:rows], last):
        block = narrow(unit_rows(dot(other, head[...], 1, 0))[0])
        total = total + dot(negatives(txt_b, block, numbers), block, 1, 0)
    text_grad[...] = narrow(off_unit(total, unit, inverse))
    token[...] = inverse[: token.shape[0]] + jnp.zeros(token.shape, token.dtype)


def image_grad_kernel(numbers, core, grads, far, unit, inverse, img_b, head, image_grad, token):
    block = rounded_unit(far[...])
    total = dot(negatives(img_b[...], block, numbers), block, 1, 0)
    extra = jnp.where(core[0] == 0, off_unit(total, unit[...], inverse[:, :1]), jnp.float32(0.0))
    grad = narrow(grads[: block.shape[0]].astype(jnp.float32) + extra)
    image_grad[...] = narrow(dot(grad, head[...], 1, 1))
    token[...] = inverse[: token.shape[0]]


def pick_kernel(core, pair, pair_p, picked):
    half, width = picked.shape[0] // 8, pair.shape[1]
    row = lax.broadcasted_iota(jnp.int32, (picked.shape[0], width), 0)
    column = lax.broadcasted_iota(jnp.int32, (picked.shape[0], width), 1)
    wanted = row + (row // half + core[0]) * half
    pick = jnp.where(column == wanted, jnp.float32(1.0), jnp.float32(0.0)).astype(jnp.bfloat16)
    count = pair.shape[0] // 2
    far = jnp.where(core[0] == 0, pair[:count], pair_p[:count])
    for index, block in enumerate((pair[count:], pair_p[count:], far)):
        picked[:, index * count : (index + 1) * count] = narrow(dot(pick, block, 1, 1))


def near_term_kernel(core, picked, grads, here, total):
    count = grads.shape[0] // 2
    total[...] = dot(picked[:, :count], grads[:count], 1, 0)


def term_kernel(core, picked, grads, grads_p, total, out):
    count, half = grads.shape[0] // 2, out.shape[1]
    far = jnp.where(core[0] == 0, grads[count:], grads_p[count:])
    term = total[...] + dot(picked[:, count : 2 * count], grads_p[:count], 1, 0)
    term = term + dot(picked[:, 2 * count :], far, 1, 0)
    for index in range(out.shape[0]):
        out[index] = narrow(term[index * half : (index + 1) * half])


def group_kernel(term, here, out):
    total = term[0].astype(jnp.float32)
    for index in range(1, term.shape[0]):
        total = total + term[index].astype(jnp.float32)
    rows, third = out.shape[1:]
    groups = total.shape[0] // rows
    for group in range(groups):
        for part in range(3):
            piece = total[group * rows : (group + 1) * rows, part * third : (part + 1) * third]
            out[group * 3 + part] = narrow(piece)
    for index in range(groups * 3, out.shape[0]):
        out[index] = jnp.zeros((rows, third), out.dtype)


def copies_kernel(pieces, here, out):
    total = pieces[0].astype(jnp.float32)
    for index in range(1, pieces.shape[0]):
        total = total + pieces[index].astype(jnp.float32)
    for index in range(out.shape[0]):
        out[index] = narrow(total)


def join_kernel(pieces, out):
    rows, third = pieces.shape[1:]
    for group in range(out.shape[0] // rows):
        row = [pieces[group * 3 + part].astype(jnp.float32) for part in range(3)]
        out[group * rows : (group + 1) * rows] = jnp.concatenate(row, 1)


def last_kernel(core, rows, rows_p, out):
    half = rows.shape[0]
    first, second = rows[...], rows_p[...].astype(jnp.float32)
    out[:half] = jnp.where(core[0] == 0, first, second)
    out[half:] = jnp.where(core[0] == 0, second, first)


def call(kernel, scalars, arrays, outs, flops, after=()):
    smem, vmem = pl.BlockSpec(memory_space=pltpu.SMEM), pl.BlockSpec(memory_space=pltpu.VMEM)
    moved = sum(a.size * a.dtype.itemsize for a in list(arrays) + list(outs))
    return pl.pallas_call(
        kernel,
        out_shape=outs if len(outs) > 1 else outs[0],
        in_specs=[smem] * len(scalars) + [vmem] * len(arrays) + [pl.BlockSpec(memory_space=pl.ANY)] * len(after),
        out_specs=[vmem] * len(outs) if len(outs) > 1 else vmem,
        compiler_params=pltpu.CompilerParams(vmem_limit_bytes=16 * 1024 * 1024),
        cost_estimate=pl.CostEstimate(flops=flops, bytes_accessed=moved, transcendentals=0),
    )(*scalars, *arrays, *after)


def per_device(images, texts, head, scale, bias, offsets):
    rows, width = images.shape
    share = head.shape[0]
    half = share // 2
    core = lax.axis_index("core")
    numbers = jnp.concatenate([scale, bias])
    pair_flops = 4 * rows * rows * width
    full_flops = 2 * rows * width * width
    wide = jax.ShapeDtypeStruct((rows, width), jnp.float32)
    slim = jax.ShapeDtypeStruct((rows, width), jnp.bfloat16)

    mine = lax.convert_element_type(core, jnp.int32).reshape(1)
    text_a = lax.ppermute(texts, DP, by_chip(1))
    image_a = lax.ppermute(images, DP, by_chip(-1))
    twice = jax.ShapeDtypeStruct((2 * rows, width), jnp.bfloat16)
    image_pair = call(stack_kernel, (), (image_a, images), (twice,), rows)
    image_pair_p = lax.ppermute(image_pair, "core", SWAP)
    units, onward = call(turn_kernel, (mine,), (texts, text_a, image_a), (twice, slim), CHAIN)
    units_p = lax.ppermute(units, "core", SWAP)
    far = lax.ppermute(onward, DP, FAR)

    y_lo = lax.axis_index("yl")
    across = lax.ppermute(head, ("core", "yl"), CROSS)
    crossed = lax.convert_element_type(core != y_lo, jnp.int32).reshape(1)
    copies = call(
        head_kernel,
        (crossed,),
        (head, across),
        (jax.ShapeDtypeStruct((4, share, width), jnp.bfloat16),),
        2 * CHAIN,
    )
    halves = exchange(copies, "x")
    other = lax.ppermute(halves, "core", SWAP)

    picked = call(
        pick_kernel,
        (mine,),
        (image_pair, image_pair_p),
        (jax.ShapeDtypeStruct((width // 2, 3 * rows), jnp.bfloat16),),
        CHAIN,
    )
    slight = jax.ShapeDtypeStruct((rows, 128), jnp.float32)
    full_head, unit, inverse, img_b, far_unit, far_inverse, far_b, partial = call(
        first_kernel,
        (numbers, offsets, mine),
        (image_pair, halves, other, units),
        (jax.ShapeDtypeStruct((width, width), jnp.bfloat16), wide, slight, slim, wide, slight, slim, wide),
        CHAIN,
    )
    grads = call(
        grad_kernel,
        (numbers, mine),
        (units_p, unit, inverse, img_b, far_unit, far_inverse, far_b, partial),
        (jax.ShapeDtypeStruct((2 * rows, width), jnp.bfloat16),),
        rows,
        (picked,),
    )

    grads_p = lax.ppermute(grads, "core", SWAP)
    pieces = jax.ShapeDtypeStruct((32, 8, width // 3), jnp.bfloat16)
    near = call(
        near_term_kernel,
        (mine,),
        (picked, grads),
        (jax.ShapeDtypeStruct((width // 2, width), jnp.float32),),
        CHAIN // 2,
        (far,),
    )
    term = call(
        term_kernel,
        (mine,),
        (picked, grads, grads_p, near),
        (jax.ShapeDtypeStruct((8, half, width), jnp.bfloat16),),
        full_flops,
    )
    term = exchange(term, REP)
    token = jax.ShapeDtypeStruct((8, 128), jnp.float32)
    text_grad, text_done = call(
        text_kernel,
        (numbers, offsets, mine),
        (texts, img_b, full_head, image_a, image_pair_p, far),
        (slim, token),
        3 * full_flops + 4 * pair_flops,
    )
    term = call(group_kernel, (), (term,), (pieces,), term.size, (text_done,))
    term = exchange(term, RING)
    image_grad, image_done = call(
        image_grad_kernel,
        (numbers, mine),
        (grads, far, unit, inverse, img_b, full_head),
        (slim, token),
        full_flops + pair_flops,
    )
    copies = call(copies_kernel, (), (term,), (pieces,), term.size, (image_done,))
    done = exchange(copies, RING)
    done = call(
        join_kernel, (), (done,), (jax.ShapeDtypeStruct((half, width), jnp.float32),), done.size
    )
    done_p = lax.ppermute(narrow(done), "core", SWAP)
    head_grad = call(
        last_kernel,
        (mine,),
        (done, done_p),
        (jax.ShapeDtypeStruct((share, width), jnp.float32),),
        done.size,
    )
    return image_grad, text_grad, head_grad


def solution(mesh):
    fine = Mesh(mesh.devices.reshape(8, 4, 2, 4, 2), ALL)
    in_specs = (P(ALL, None), P(ALL, None), P(REP, None), P(), P(), P(ALL))
    out_specs = (P(ALL, None), P(ALL, None), P(REP, None))
    return jax.shard_map(
        per_device, mesh=fine, in_specs=in_specs, out_specs=out_specs, check_vma=False
    )
```

```python
import jax
import jax.numpy as jnp
from jax import lax
from jax.experimental import pallas as pl
from jax.experimental.pallas import tpu as pltpu
from jax.sharding import Mesh
from jax.sharding import PartitionSpec as P

EPS = 1e-06
CHAIN = 20_000_000_000
DP = ("z", "yh", "core")
RING = ("z", "yh")
REP = ("x", "yl")
ALL = DP + REP


def dot(a, b, ca, cb):
    return lax.dot_general(a, b, (((ca,), (cb,)), ((), ())), preferred_element_type=jnp.float32)


def by_chip(shift):
    return [(p, (p + 2 * shift) % 64) for p in range(64)]


SWAP = [(0, 1), (1, 0)]
CROSS = [(0, 1), (3, 2)]
FAR = [(p, (p + (1 if p % 2 else 63)) % 64) for p in range(64)]


def exchange(array, axes):
    return lax.all_to_all(array, axes, split_axis=0, concat_axis=0, tiled=True)


def unit_rows(values):
    inverse = lax.rsqrt(jnp.sum(values * values, axis=-1, keepdims=True) + EPS)
    return values * inverse, inverse


def off_unit(direction, unit, inverse):
    return (direction - unit * jnp.sum(unit * direction, axis=-1, keepdims=True)) * inverse


def narrow(values):
    return values.astype(jnp.bfloat16)


def rounded_unit(block):
    return narrow(unit_rows(block.astype(jnp.float32))[0])


def negatives(a, b, numbers):
    logits = numbers[0] * dot(a, b, 1, 1) + numbers[1]
    return narrow(numbers[0] * jax.nn.sigmoid(logits))


def own_pairs(a, b, numbers, positive):
    logits = numbers[0] * dot(a, b, 1, 1) + numbers[1]
    sign = jnp.where(positive, jnp.float32(1.0), jnp.float32(-1.0))
    return narrow(numbers[0] * (-sign * jax.nn.sigmoid(-sign * logits)))


def positives(offset, rows, image_dim):
    image = lax.broadcasted_iota(jnp.int32, (rows, rows), image_dim)
    text = lax.broadcasted_iota(jnp.int32, (rows, rows), 1 - image_dim)
    target = image + offset
    return text == jnp.where(target >= rows, target - rows, target)


def head_kernel(crossed, head, across, copies):
    shard = jnp.where(crossed[0] == 1, across[...], head[...])
    for index in range(copies.shape[0]):
        copies[index] = shard


def turn_kernel(core, texts, text_a, image_a, units, onward):
    rows = texts.shape[0]
    units[:rows] = rounded_unit(text_a[...])
    units[rows:] = rounded_unit(texts[...])
    onward[...] = jnp.where(core[0] == 0, image_a[...], text_a[...])


def stack_kernel(first, second, out):
    rows = first.shape[0]
    out[:rows] = first[...]
    out[rows:] = second[...]


def first_kernel(
    numbers, offset, core, pair, halves, other, units,
    head, unit, inverse, img_b, far_unit, far_inverse, far_b, partial,
):
    count, share = halves.shape[:2]
    for index in range(count):
        for source, place in ((halves, core[0]), (other, 1 - core[0])):
            start = pl.multiple_of((2 * index + place) * share, 16)
            head[pl.ds(start, share), :] = source[index]

    rows = img_b.shape[0]
    units_all, inverse_all = unit_rows(dot(pair[...], head[...], 1, 0))
    rounded = narrow(units_all[rows:])
    unit[...] = units_all[rows:]
    inverse[...] = jnp.broadcast_to(inverse_all[rows:], inverse.shape)
    img_b[...] = rounded

    def keep(value, inverse_value):
        far_unit[...] = value
        far_inverse[...] = jnp.broadcast_to(inverse_value, far_inverse.shape)
        far_b[...] = narrow(value)

    @pl.when(core[0] == 0)
    def _():
        keep(units_all[:rows], inverse_all[:rows])

    @pl.when(core[0] != 0)
    def _():
        keep(units_all[rows:], inverse_all[rows:])

    block = units[rows:]
    weights = own_pairs(rounded, block, numbers, positives(offset[0], rows, 0))
    total = dot(weights, block, 1, 0)
    block = units[:rows]
    partial[...] = total + dot(negatives(rounded, block, numbers), block, 1, 0)


def grad_kernel(
    numbers, core, units_p, unit, inverse, img_b, far_unit, far_inverse, far_b, partial, here,
    grads,
):
    rows = img_b.shape[0]
    block = units_p[:rows]
    total = partial[...] + dot(negatives(img_b[...], block, numbers), block, 1, 0)
    grad = off_unit(total, unit[...], inverse[:, :1])
    far = jnp.where(core[0] == 0, block, units_p[rows:])
    total = dot(negatives(far_b[...], far, numbers), far, 1, 0)
    far_grad = off_unit(total, far_unit[...], far_inverse[:, :1])

    @pl.when(core[0] == 0)
    def _():
        grads[:rows] = narrow(grad)
        grads[rows:] = narrow(far_grad)

    @pl.when(core[0] != 0)
    def _():
        grads[:rows] = narrow(grad + far_grad)
        grads[rows:] = jnp.zeros_like(far_grad, grads.dtype)


def text_kernel(numbers, offset, core, texts, img_b, head, image_a, pair_p, far, text_grad, token):
    unit, inverse = unit_rows(texts[...].astype(jnp.float32))
    txt_b = narrow(unit)
    own = img_b[...]
    weights = own_pairs(txt_b, own, numbers, positives(offset[0], own.shape[0], 1))
    total = dot(weights, own, 1, 0)
    rows = own.shape[0]
    last = jnp.where(core[0] == 0, pair_p[rows:], far[...])
    for other in (image_a[...], pair_p[:rows], last):
        block = narrow(unit_rows(dot(other, head[...], 1, 0))[0])
        total = total + dot(negatives(txt_b, block, numbers), block, 1, 0)
    text_grad[...] = narrow(off_unit(total, unit, inverse))
    token[...] = inverse[: token.shape[0]] + jnp.zeros(token.shape, token.dtype)


def image_grad_kernel(numbers, core, grads, far, unit, inverse, img_b, head, image_grad, token):
    block = rounded_unit(far[...])
    total = dot(negatives(img_b[...], block, numbers), block, 1, 0)
    extra = jnp.where(core[0] == 0, off_unit(total, unit[...], inverse[:, :1]), jnp.float32(0.0))
    grad = narrow(grads[: block.shape[0]].astype(jnp.float32) + extra)
    image_grad[...] = narrow(dot(grad, head[...], 1, 1))
    token[...] = inverse[: token.shape[0]]


def pick_kernel(core, pair, pair_p, picked):
    half, width = picked.shape[0] // 8, pair.shape[1]
    row = lax.broadcasted_iota(jnp.int32, (picked.shape[0], width), 0)
    column = lax.broadcasted_iota(jnp.int32, (picked.shape[0], width), 1)
    wanted = row + (row // half + core[0]) * half
    pick = jnp.where(column == wanted, jnp.float32(1.0), jnp.float32(0.0)).astype(jnp.bfloat16)
    count = pair.shape[0] // 2
    far = jnp.where(core[0] == 0, pair[:count], pair_p[:count])
    for index, block in enumerate((pair[count:], pair_p[count:], far)):
        picked[:, index * count : (index + 1) * count] = narrow(dot(pick, block, 1, 1))


def near_term_kernel(core, picked, grads, here, total):
    count = grads.shape[0] // 2
    total[...] = dot(picked[:, :count], grads[:count], 1, 0)


def term_kernel(core, picked, grads, grads_p, total, out):
    count, half = grads.shape[0] // 2, out.shape[1]
    far = jnp.where(core[0] == 0, grads[count:], grads_p[count:])
    term = total[...] + dot(picked[:, count:], jnp.concatenate([grads_p[:count], far], 0), 1, 0)
    for index in range(out.shape[0]):
        out[index] = narrow(term[index * half : (index + 1) * half])


def group_kernel(term, here, out):
    total = term[0].astype(jnp.float32)
    for index in range(1, term.shape[0]):
        total = total + term[index].astype(jnp.float32)
    rows, third = out.shape[1:]
    groups = total.shape[0] // rows
    for group in range(groups):
        for part in range(3):
            piece = total[group * rows : (group + 1) * rows, part * third : (part + 1) * third]
            out[group * 3 + part] = narrow(piece)
    for index in range(groups * 3, out.shape[0]):
        out[index] = jnp.zeros((rows, third), out.dtype)


def copies_kernel(pieces, here, out):
    total = pieces[0].astype(jnp.float32)
    for index in range(1, pieces.shape[0]):
        total = total + pieces[index].astype(jnp.float32)
    for index in range(out.shape[0]):
        out[index] = narrow(total)


def join_kernel(pieces, out):
    rows, third = pieces.shape[1:]
    for group in range(out.shape[0] // rows):
        row = [pieces[group * 3 + part].astype(jnp.float32) for part in range(3)]
        out[group * rows : (group + 1) * rows] = jnp.concatenate(row, 1)


def last_kernel(core, rows, rows_p, out):
    half = rows.shape[0]
    first, second = rows[...], rows_p[...].astype(jnp.float32)
    out[:half] = jnp.where(core[0] == 0, first, second)
    out[half:] = jnp.where(core[0] == 0, second, first)


def call(kernel, scalars, arrays, outs, flops, after=()):
    smem, vmem = pl.BlockSpec(memory_space=pltpu.SMEM), pl.BlockSpec(memory_space=pltpu.VMEM)
    moved = sum(a.size * a.dtype.itemsize for a in list(arrays) + list(outs))
    return pl.pallas_call(
        kernel,
        out_shape=outs if len(outs) > 1 else outs[0],
        in_specs=[smem] * len(scalars) + [vmem] * len(arrays) + [pl.BlockSpec(memory_space=pl.ANY)] * len(after),
        out_specs=[vmem] * len(outs) if len(outs) > 1 else vmem,
        compiler_params=pltpu.CompilerParams(vmem_limit_bytes=16 * 1024 * 1024),
        cost_estimate=pl.CostEstimate(flops=flops, bytes_accessed=moved, transcendentals=0),
    )(*scalars, *arrays, *after)


def per_device(images, texts, head, scale, bias, offsets):
    rows, width = images.shape
    share = head.shape[0]
    half = share // 2
    core = lax.axis_index("core")
    numbers = jnp.concatenate([scale, bias])
    pair_flops = 4 * rows * rows * width
    full_flops = 2 * rows * width * width
    wide = jax.ShapeDtypeStruct((rows, width), jnp.float32)
    slim = jax.ShapeDtypeStruct((rows, width), jnp.bfloat16)

    mine = lax.convert_element_type(core, jnp.int32).reshape(1)
    text_a = lax.ppermute(texts, DP, by_chip(1))
    image_a = lax.ppermute(images, DP, by_chip(-1))
    twice = jax.ShapeDtypeStruct((2 * rows, width), jnp.bfloat16)
    image_pair = call(stack_kernel, (), (image_a, images), (twice,), rows)
    image_pair_p = lax.ppermute(image_pair, "core", SWAP)
    units, onward = call(turn_kernel, (mine,), (texts, text_a, image_a), (twice, slim), CHAIN)
    units_p = lax.ppermute(units, "core", SWAP)
    far = lax.ppermute(onward, DP, FAR)

    y_lo = lax.axis_index("yl")
    across = lax.ppermute(head, ("core", "yl"), CROSS)
    crossed = lax.convert_element_type(core != y_lo, jnp.int32).reshape(1)
    copies = call(
        head_kernel,
        (crossed,),
        (head, across),
        (jax.ShapeDtypeStruct((4, share, width), jnp.bfloat16),),
        2 * CHAIN,
    )
    halves = exchange(copies, "x")
    other = lax.ppermute(halves, "core", SWAP)

    picked = call(
        pick_kernel,
        (mine,),
        (image_pair, image_pair_p),
        (jax.ShapeDtypeStruct((width // 2, 3 * rows), jnp.bfloat16),),
        CHAIN,
    )
    slight = jax.ShapeDtypeStruct((rows, 128), jnp.float32)
    full_head, unit, inverse, img_b, far_unit, far_inverse, far_b, partial = call(
        first_kernel,
        (numbers, offsets, mine),
        (image_pair, halves, other, units),
        (jax.ShapeDtypeStruct((width, width), jnp.bfloat16), wide, slight, slim, wide, slight, slim, wide),
        CHAIN,
    )
    grads = call(
        grad_kernel,
        (numbers, mine),
        (units_p, unit, inverse, img_b, far_unit, far_inverse, far_b, partial),
        (jax.ShapeDtypeStruct((2 * rows, width), jnp.bfloat16),),
        rows,
        (picked,),
    )

    grads_p = lax.ppermute(grads, "core", SWAP)
    pieces = jax.ShapeDtypeStruct((32, 8, width // 3), jnp.bfloat16)
    near = call(
        near_term_kernel,
        (mine,),
        (picked, grads),
        (jax.ShapeDtypeStruct((width // 2, width), jnp.float32),),
        CHAIN // 2,
        (far,),
    )
    term = call(
        term_kernel,
        (mine,),
        (picked, grads, grads_p, near),
        (jax.ShapeDtypeStruct((8, half, width), jnp.bfloat16),),
        full_flops,
    )
    term = exchange(term, REP)
    token = jax.ShapeDtypeStruct((8, 128), jnp.float32)
    text_grad, text_done = call(
        text_kernel,
        (numbers, offsets, mine),
        (texts, img_b, full_head, image_a, image_pair_p, far),
        (slim, token),
        3 * full_flops + 4 * pair_flops,
    )
    term = call(group_kernel, (), (term,), (pieces,), term.size, (text_done,))
    term = exchange(term, RING)
    image_grad, image_done = call(
        image_grad_kernel,
        (numbers, mine),
        (grads, far, unit, inverse, img_b, full_head),
        (slim, token),
        full_flops + pair_flops,
    )
    copies = call(copies_kernel, (), (term,), (pieces,), term.size, (image_done,))
    done = exchange(copies, RING)
    done = call(
        join_kernel, (), (done,), (jax.ShapeDtypeStruct((half, width), jnp.float32),), done.size
    )
    done_p = lax.ppermute(narrow(done), "core", SWAP)
    head_grad = call(
        last_kernel,
        (mine,),
        (done, done_p),
        (jax.ShapeDtypeStruct((share, width), jnp.float32),),
        done.size,
    )
    return image_grad, text_grad, head_grad


def solution(mesh):
    fine = Mesh(mesh.devices.reshape(8, 4, 2, 4, 2), ALL)
    in_specs = (P(ALL, None), P(ALL, None), P(REP, None), P(), P(), P(ALL))
    out_specs = (P(ALL, None), P(ALL, None), P(REP, None))
    return jax.shard_map(
        per_device, mesh=fine, in_specs=in_specs, out_specs=out_specs, check_vma=False
    )
```
